256 devices in a mesh: tm: 16 (over y, x), tile: 16 (over z, core).
Axes of the slice: x: 4, y: 4, z: 8, core: 2. Of those that a mesh axis runs over, the one named last changes fastest.
Arguments:
- activations: bfloat16 [128, 64, 16, 256], P('tm', 'tile'), may hold values from -6 to 6
- grad_output: bfloat16 [128, 128, 32, 128], P('tm', 'tile'), may hold values from -6 to 6
- conv_weight: bfloat16 [27, 256, 128], replicated, may hold values from -0.078125 to 0.078125
- frame_counts: int32 [16], P('tm'), may hold values from 2 to 8, as said below
Outputs:
- grad_input: bfloat16 [128, 64, 16, 256], P('tm', 'tile')
- grad_weight: float32 [27, 256, 128], replicated
The draws below stay inside these ranges and needn't reach their ends.
Inputs may be any that keep to these rules, and one draw needn't show every extreme that they name: `frame_counts`: every device uses at least 2 of its 8 slots, and in every draw some device uses all 8.
All inputs are finite; a program needn't handle non-finite values.
Results may differ from the reference program's by a relative error of at most 0.001.
Values may be sent and summed in bfloat16 or wider, within the bound.
No kernel may reach another device: no remote copies, remote signals or barrier semaphores. Data moves between devices by JAX's collectives and lax.ppermute only.
A program may use at most 192 MiB of HBM per device.

```python
import math
import jax
import jax.numpy as jnp
from jax import lax

CIN = 256
COUT = 128
CAP = 8
WL = 16
FRAME_SLOTS = 128
NH = 64
FULL_POS = 524288
N_TM = 16


def draw_frame_counts(key, part):
    key = jax.random.fold_in(key, 7)
    first_key, second_key = jax.random.split(key)
    counts_drawn = jax.random.randint(first_key, (N_TM,), 2, CAP + 1)
    fullest = jax.random.randint(second_key, (), 0, N_TM)
    return counts_drawn.at[fullest].set(CAP).astype(jnp.int32)


def block_scale(stream_key, shape, shards, smallest, high):
    def one(axis_at, blocks):
        draws = jax.random.uniform(jax.random.fold_in(jax.random.fold_in(stream_key, 6), axis_at), (blocks,), jnp.float32, smallest / len(shards), high / len(shards))
        return jnp.repeat(jnp.exp(draws), shape[axis_at] // blocks).reshape((-1,) + (1,) * (len(shape) - axis_at - 1))

    factor_of = one(*shards[0])
    for cut in shards[1:]:
        factor_of = factor_of * one(*cut)
    return factor_of


def normal_values(own_key, dims, spread, most, cuts=(), kind=jnp.bfloat16):
    level = block_scale(own_key, dims, cuts, -0.22, 0.18) if cuts else 1.0
    values = jax.random.normal(own_key, dims, jnp.float32) * spread * level
    return jnp.minimum(jnp.maximum(values, -most), most).astype(kind)


def setup_inputs(seed: int = 0) -> dict:
    streams_of = jax.random.split(jax.random.key(seed), 5)
    return {
        "activations": normal_values(streams_of[0], (FRAME_SLOTS, NH, WL, CIN), 1.0, 6.0, ((0, 16), (1, 16))),
        "grad_output": normal_values(streams_of[1], (FRAME_SLOTS, 2 * NH, 2 * WL, COUT), 1.0, 6.0, ((0, 16), (1, 16))),
        "conv_weight": normal_values(streams_of[2], (27, CIN, COUT), (27 * CIN) ** -0.5, 0.078125),
        "frame_counts": draw_frame_counts(jax.random.fold_in(streams_of[4], 71), 0),
    }


def reference(activations, grad_output, conv_weight, frame_counts):
    slot_total = FRAME_SLOTS
    used = frame_counts.astype(jnp.int32)
    starts = jnp.cumsum(used) - used
    clip_frames = jnp.sum(used)
    position = jnp.arange(slot_total, dtype=jnp.int32)
    owner = lax.optimization_barrier(jnp.sum((position[:, None] >= starts[None, :]).astype(jnp.int32), axis=1)) - 1
    source = owner * CAP + position - starts[owner]
    valid = position < clip_frames
    source = jnp.where(valid, source, 0).astype(jnp.int32)
    packed_x = jnp.where(valid[:, None, None, None], activations[source], jnp.zeros((), jnp.bfloat16))
    packed_g = jnp.where(valid[:, None, None, None], grad_output[source], jnp.zeros((), jnp.bfloat16))
    upsampled = jnp.repeat(jnp.repeat(packed_x, 2, axis=1), 2, axis=2)
    u_padded = jnp.pad(upsampled, ((2, 0), (1, 1), (1, 1), (0, 0)))
    g_padded = jnp.pad(packed_g, ((0, 2), (1, 1), (1, 1), (0, 0)))
    high = 2 * NH
    wide = 2 * WL
    flat_count = slot_total * high * wide
    g_flat = packed_g.reshape(flat_count, COUT)
    weight_terms = []
    grad_up = jnp.zeros((flat_count, CIN), jnp.float32)
    for depth_tap in range(3):
        for row_tap in range(3):
            for col_tap in range(3):
                tap_index = 9 * depth_tap + 3 * row_tap + col_tap
                u_piece = u_padded[depth_tap:depth_tap + slot_total, row_tap:row_tap + high, col_tap:col_tap + wide]
                u_piece = u_piece.reshape(flat_count, CIN)
                weight_terms.append(jnp.dot(jnp.transpose(u_piece), g_flat, preferred_element_type=jnp.float32))
                g_piece = g_padded[2 - depth_tap:2 - depth_tap + slot_total, 2 - row_tap:2 - row_tap + high, 2 - col_tap:2 - col_tap + wide]
                g_piece = g_piece.reshape(flat_count, COUT)
                grad_up = grad_up + jnp.dot(g_piece, jnp.transpose(conv_weight[tap_index]), preferred_element_type=jnp.float32)
    grad_weight = jnp.stack(weight_terms, axis=0) * (1.0 / math.sqrt(FULL_POS))
    blocked = grad_up.reshape(slot_total, NH, 2, WL, 2, CIN)
    grad_packed = lax.optimization_barrier(jnp.sum(blocked, axis=(2, 4)))
    slot_owner = position // CAP
    slot_within = position % CAP
    target = starts[slot_owner] + slot_within
    alive = slot_within < used[slot_owner]
    target = jnp.minimum(target, slot_total - 1).astype(jnp.int32)
    grad_input = jnp.where(alive[:, None, None, None], grad_packed[target], jnp.zeros((), jnp.float32))
    return (grad_input.astype(jnp.bfloat16), grad_weight)
```

```python
import math

import jax
import jax.numpy as jnp
import numpy as np
from jax import lax
from jax.experimental import pallas as pl
from jax.experimental.pallas import tpu as pltpu
from jax.sharding import PartitionSpec as P

BOTH = ("tm", "tile")
F32 = jnp.float32
BF16 = jnp.bfloat16
F16 = jnp.float16


def moved(rank, kind, step):
    tm, tile = divmod(rank, 16)
    y, x = divmod(tm, 4)
    z, core = divmod(tile, 2)
    if kind == "core":
        core ^= 1
    elif kind == "z":
        z ^= step
    elif (kind == "first") == (core == 0):
        x ^= step
    else:
        y ^= step
    return (y * 4 + x) * 16 + z * 2 + core


def swapped(value, kind, step=1):
    return lax.ppermute(value, BOTH, [(rank, moved(rank, kind, step)) for rank in range(256)])


def shifted(value, tm_step, tile_step):
    pairs = []
    for rank in range(256):
        tm, tile = divmod(rank, 16)
        tm, tile = tm + tm_step, tile + tile_step
        if 0 <= tm < 16 and 0 <= tile < 16:
            pairs.append((rank, tm * 16 + tile))
    return lax.ppermute(value, BOTH, pairs)


def power(exponent):
    whole = exponent.astype(jnp.int32)
    size = jnp.abs(whole)
    result = jnp.ones_like(exponent)
    for bit in range(7):
        factor = jnp.where(whole >= 0, F32(2.0 ** (2**bit)), F32(2.0 ** -(2**bit)))
        result = result * jnp.where((size >> bit) & 1 == 1, factor, F32(1))
    return lax.optimization_barrier(result)


def packed(value, exponent, scale):
    tail = jnp.broadcast_to(exponent.astype(F16), (8, 128))
    return jnp.concatenate([(value * scale).astype(F16), tail], axis=0)


def opened(message):
    exponent = message[-8:-7].astype(F32)
    return message[:-8].astype(F32) * power(-exponent), exponent


def scattered(total, exponent, place, kind):
    rows = total.shape[0] // 4
    scale = power(exponent)
    parts = []
    lowest = exponent
    for step in (1, 3, 2):
        piece = lax.dynamic_slice_in_dim(total, (place ^ step) * rows, rows, 0)
        part, theirs = opened(swapped(packed(piece, exponent, scale), kind, step))
        parts.append(part)
        lowest = jnp.minimum(lowest, theirs)
    mine = lax.dynamic_slice_in_dim(total, place * rows, rows, 0)
    return (mine + parts[0]) + (parts[1] + parts[2]), lowest - 2


def gathered(message, place, kind):
    buffer = jnp.zeros((4,) + message.shape, F16)
    for step in (0, 1, 3, 2):
        theirs = swapped(message, kind, step) if step else message
        buffer = lax.dynamic_update_index_in_dim(buffer, theirs, place ^ step, 0)
    return buffer.reshape((-1,) + message.shape[-2:])


def summed_everywhere(own, received, bound, factor):
    tm, tile = lax.axis_index("tm"), lax.axis_index("tile")
    y, x, core = tm // 4, tm % 4, tile % 2
    first = jnp.where(core == 0, x, y)
    second = jnp.where(core == 0, y, x)
    exponent = jnp.floor(13 - jnp.log2(jnp.maximum(bound, F32(1e-30))))
    total, exponent = scattered(own + received, exponent, first, "first")
    total, exponent = scattered(total, exponent, second, "second")
    for steps in ((1,), (2, 4, 6)):
        message = packed(total, exponent, power(exponent))
        parts = [opened(message)] + [opened(swapped(message, "z", step)) for step in steps]
        while len(parts) > 1:
            parts = [
                (a + b, jnp.minimum(e, f) - 1)
                for (a, e), (b, f) in zip(parts[::2], parts[1::2])
            ]
        total, exponent = parts[0]
    message = packed(total, exponent, power(exponent))[None]
    message = gathered(message, second, "second")
    message = gathered(message, first, "first")
    other = swapped(message, "core")

    def restored(pieces):
        scale = power(-pieces[:, -8:-7].astype(F32)) * F32(factor)
        return pieces[:, :-8].astype(F32) * scale

    mine, theirs = restored(message), restored(other)
    return jnp.stack([jnp.where(core == 0, mine, theirs), jnp.where(core == 0, theirs, mine)])


def box_matrix():
    box = np.zeros((9, 4, 16, 320), np.float32)
    for dh in range(3):
        for dw in range(3):
            for i in range(4):
                for j in range(16):
                    for h in (2 * i + 1 - dh, 2 * i + 2 - dh):
                        for w in (2 * j + 1 - dw, 2 * j + 2 - dw):
                            if 0 <= w < 32:
                                row = 256 if h < 0 else 288 if h > 7 else 32 * h
                                box[3 * dh + dw, i, j, row + w] = 1
    return box.reshape(576, 320)


def weight_kernel(
    info, x_ref, g_ref, top_ref, bottom_ref, later_ref, later_top_ref, later_bottom_ref, box_ref,
    own_ref, sent_ref, bound_ref, high_ref, low_ref, frames, terms,
):
    used, core = info[0], info[1]
    frames[0:8, 0:256] = g_ref[...]
    frames[0:8, 256:288] = top_ref[...]
    frames[0:8, 288:320] = bottom_ref[...]
    frames[8:10] = jnp.zeros((2, 320, 128), BF16)
    for k in range(2):
        frames[used + k, 0:256] = later_ref[k]
        frames[used + k, 256:288] = later_top_ref[k]
        frames[used + k, 288:320] = later_bottom_ref[k]
    for pair in range(5):
        two = jnp.concatenate([frames[2 * pair], frames[2 * pair + 1]], axis=1)
        sums = jnp.dot(box_ref[...], two, preferred_element_type=F32)
        high = sums.astype(BF16)
        low = (sums - high.astype(F32)).astype(BF16)
        for k in range(2):
            rows = slice(64 * (2 * pair + k), 64 * (2 * pair + k + 1))
            for tap in range(9):
                block = (slice(64 * tap, 64 * tap + 64), slice(128 * k, 128 * k + 128))
                high_ref[rows, 128 * tap : 128 * tap + 128] = high[block]
                low_ref[rows, 128 * tap : 128 * tap + 128] = low[block]
    slot = lax.broadcasted_iota(jnp.int32, (512, 256), 0) // 64
    x = jnp.where(slot < used, x_ref[...], jnp.zeros((), BF16)).T
    for dt in range(3):
        rows = slice(64 * (2 - dt), 64 * (2 - dt) + 512)
        for at in range(0, 1152, 256):
            columns = slice(at, min(at + 256, 1152))
            term = jnp.dot(x, high_ref[rows, columns], preferred_element_type=F32)
            term = term + jnp.dot(x, low_ref[rows, columns], preferred_element_type=F32)
            for k in range(0, term.shape[1], 128):
                tap = 9 * dt + (at + k) // 128
                terms[256 * tap : 256 * tap + 256] = term[:, k : k + 128]
    own = terms[pl.ds(pl.multiple_of(core * 3456, 8), 3456)]
    own_ref[...] = own
    sent = terms[pl.ds(pl.multiple_of((1 - core) * 3456, 8), 3456)]
    sent_ref[0:3456] = sent
    bound_ref[...] = jnp.broadcast_to(jnp.max(jnp.abs(own)), (8, 128))
    sent_ref[3456:3464] = jnp.broadcast_to(jnp.max(jnp.abs(sent)), (8, 128))


def input_kernel(info, high_ref, low_ref, weight_ref, out_ref):
    total = jnp.zeros((512, 256), F32)
    for dt in range(3):
        rows = slice(64 * (2 - dt), 64 * (2 - dt) + 512)
        weight = weight_ref[1152 * dt : 1152 * dt + 1152]
        total = total + jnp.dot(high_ref[rows], weight, preferred_element_type=F32)
        total = total + jnp.dot(low_ref[rows], weight, preferred_element_type=F32)
    slot = lax.broadcasted_iota(jnp.int32, (512, 256), 0) // 64
    out_ref[...] = jnp.where(slot < info[0], total, F32(0)).astype(BF16)


def shards(activations, grad_output, conv_weight, frame_counts):
    info = jnp.concatenate([frame_counts, (lax.axis_index("tile") % 2)[None].astype(jnp.int32)])
    cotangent = grad_output.reshape(8, 256, 128)
    first_row, last_row = cotangent[:, :32], cotangent[:, 224:]
    with jax.named_scope("edges"):
        top = shifted(last_row, 0, 1)
        bottom = shifted(first_row, 0, -1)
        later = shifted(cotangent[:2], -1, 0)
        later_top = shifted(last_row[:2], -1, 1)
        later_bottom = shifted(first_row[:2], -1, -1)
    whole = pl.BlockSpec(memory_space=pltpu.VMEM)
    scalars = pl.BlockSpec(memory_space=pltpu.SMEM)
    with jax.named_scope("weight_terms"):
        own, sent, bound, high, low = pl.pallas_call(
            weight_kernel,
            out_shape=(
                jax.ShapeDtypeStruct((3456, 128), F32),
                jax.ShapeDtypeStruct((3464, 128), F32),
                jax.ShapeDtypeStruct((8, 128), F32),
                jax.ShapeDtypeStruct((640, 1152), BF16),
                jax.ShapeDtypeStruct((640, 1152), BF16),
            ),
            in_specs=[scalars] + [whole] * 8,
            out_specs=(whole,) * 5,
            scratch_shapes=[pltpu.VMEM((10, 320, 128), BF16), pltpu.VMEM((6912, 128), F32)],
            compiler_params=pltpu.CompilerParams(vmem_limit_bytes=40 * 2**20),
            cost_estimate=pl.CostEstimate(
                flops=3 * 10**9, bytes_accessed=10**7, transcendentals=0
            ),
        )(
            info, activations.reshape(512, 256), cotangent, top, bottom, later, later_top,
            later_bottom, jnp.asarray(box_matrix(), BF16),
        )
    with jax.named_scope("halves"):
        received = swapped(sent, "core")
    weight = jnp.transpose(conv_weight, (0, 2, 1)).reshape(3456, 256)
    with jax.named_scope("input_terms"):
        grad_input = pl.pallas_call(
            input_kernel,
            out_shape=jax.ShapeDtypeStruct((512, 256), BF16),
            in_specs=[scalars] + [whole] * 3,
            out_specs=whole,
            compiler_params=pltpu.CompilerParams(vmem_limit_bytes=40 * 2**20),
            cost_estimate=pl.CostEstimate(
                flops=2 * 10**9, bytes_accessed=5 * 10**6, transcendentals=0
            ),
        )(info, high, low, weight)
    with jax.named_scope("weight_sum"):
        factor = 1.0 / math.sqrt(16 * 16 * 2048)
        grad_weight = summed_everywhere(
            own, received[:3456], bound[:1] + received[3456:3457], factor
        )
    return grad_input.reshape(8, 4, 16, 256), grad_weight.reshape(27, 256, 128)


def solution(mesh):
    placed = (P("tm", "tile", None, None), P("tm", "tile", None, None), P(), P("tm"))
    return jax.shard_map(
        shards,
        mesh=mesh,
        in_specs=placed,
        out_specs=(P("tm", "tile", None, None), P()),
        check_vma=False,
    )
```

```python
import math

import jax
import jax.numpy as jnp
import numpy as np
from jax import lax
from jax.experimental import pallas as pl
from jax.experimental.pallas import tpu as pltpu
from jax.sharding import PartitionSpec as P

BOTH = ("tm", "tile")
F32 = jnp.float32
BF16 = jnp.bfloat16
F16 = jnp.float16


def moved(rank, kind, step):
    tm, tile = divmod(rank, 16)
    y, x = divmod(tm, 4)
    z, core = divmod(tile, 2)
    if kind == "core":
        core ^= 1
    elif kind == "strip":
        tile += 1 if core else -1
        return tm * 16 + tile if 0 <= tile < 16 else None
    elif kind == "pair":
        z ^= 1
    elif kind == "z":
        z = (z + step if z % 2 else z - step) % 8
    elif (kind == "first") == (core == 0):
        x ^= step
    else:
        y ^= step
    return (y * 4 + x) * 16 + z * 2 + core


def swapped(value, kind, step=1):
    pairs = [(rank, moved(rank, kind, step)) for rank in range(256)]
    return lax.ppermute(value, BOTH, [pair for pair in pairs if pair[1] is not None])


def shifted(value, tm_step, tile_step):
    pairs = []
    for rank in range(256):
        tm, tile = divmod(rank, 16)
        tm, tile = tm + tm_step, tile + tile_step
        if 0 <= tm < 16 and 0 <= tile < 16:
            pairs.append((rank, tm * 16 + tile))
    return lax.ppermute(value, BOTH, pairs)


def position():
    tm, tile = lax.axis_index("tm"), lax.axis_index("tile")
    y, x, core = tm // 4, tm % 4, tile % 2
    return core, jnp.where(core == 0, x, y), jnp.where(core == 0, y, x)


def power(exponent):
    whole = exponent.astype(jnp.int32)
    size = jnp.abs(whole)
    result = jnp.ones_like(exponent)
    for bit in range(7):
        factor = jnp.where(whole >= 0, F32(2.0 ** (2**bit)), F32(2.0 ** -(2**bit)))
        result = result * jnp.where((size >> bit) & 1 == 1, factor, F32(1))
    return lax.optimization_barrier(result)


def packed(value, exponent, scale):
    tail = jnp.broadcast_to(exponent.astype(F16), (8, 128))
    return jnp.concatenate([(value * scale).astype(F16), tail], axis=0)


def opened(message):
    exponent = message[-8:-7].astype(F32)
    return message[:-8].astype(F32) * power(-exponent), exponent


def scattered(pieces, exponent, kind, after=None):
    scale = power(exponent)
    lowest = exponent
    parts = [pieces[0]]
    arrived = [swapped(packed(pieces[step], exponent, scale), kind, step) for step in (1, 3, 2)]
    if after is not None:
        *arrived, after = lax.optimization_barrier((*arrived, after))
    for message in arrived:
        part, theirs = opened(message)
        parts.append(part)
        lowest = jnp.minimum(lowest, theirs)
    return (parts[0] + parts[1]) + (parts[2] + parts[3]), lowest - 2, after


def placed_at(buffer, piece, place):
    return lax.dynamic_update_index_in_dim(buffer, piece, place, 0)


def summed_everywhere(own, received, grad_input, factor):
    core, first, second = position()
    bound = own[3456:3457] + received[3456:3457]
    exponent = jnp.floor(13 - jnp.log2(jnp.maximum(bound, F32(1e-30))))
    pieces = [own[r : r + 864] + received[r : r + 864] for r in range(0, 3456, 864)]
    total, exponent, grad_input = scattered(pieces, exponent, "first", grad_input)
    pieces = [total[r : r + 216] for r in range(0, 864, 216)]
    total, exponent, _ = scattered(pieces, exponent, "second")
    message = packed(total, exponent, power(exponent))
    (a, e), (b, f) = opened(message), opened(swapped(message, "pair"))
    total, exponent = a + b, jnp.minimum(e, f) - 1
    message = packed(total, exponent, power(exponent))
    parts = [opened(message)] + [opened(swapped(message, "z", step)) for step in (3, 2, 1)]
    total = (parts[0][0] + parts[1][0]) + (parts[2][0] + parts[3][0])
    exponent = jnp.stack([part[1] for part in parts]).min(axis=0) - 2
    message = packed(total, exponent, power(exponent))
    row = jnp.zeros((4, 224, 128), F16)
    for step in (0, 1, 3, 2):
        theirs = swapped(message, "second", step) if step else message
        row = placed_at(row, theirs, second ^ step)
    pieces = [row] + [swapped(row, "first", step) for step in (1, 3, 2)]
    mine = theirs = jnp.zeros((4, 4, 224, 128), F16)
    for pair, steps in ((pieces[:2], (0, 1)), (pieces[2:], (3, 2))):
        other = swapped(jnp.stack(pair), "core")
        for k, step in enumerate(steps):
            mine = placed_at(mine, pair[k], first ^ step)
            theirs = placed_at(theirs, other[k], second ^ step)
    result = jnp.zeros((2, 4, 4, 216, 128), F32)
    for half, pieces in ((core, mine), (1 - core, theirs)):
        scale = power(-pieces[:, :, -8:-7].astype(F32)) * F32(factor)
        result = placed_at(result, pieces[:, :, :-8].astype(F32) * scale, half)
    return result, grad_input


def box_matrix():
    box = np.zeros((9, 4, 16, 320), np.float32)
    for dh in range(3):
        for dw in range(3):
            for i in range(4):
                for j in range(16):
                    for h in (2 * i + 1 - dh, 2 * i + 2 - dh):
                        for w in (2 * j + 1 - dw, 2 * j + 2 - dw):
                            if 0 <= w < 32:
                                row = 256 if h < 0 else 288 if h > 7 else 32 * h
                                box[3 * dh + dw, i, j, row + w] = 1
    return box.reshape(576, 320)


def box_sums(box, frame, next_frame, high_ref, low_ref, row):
    two = jnp.concatenate([frame, next_frame], axis=1)
    sums = jnp.dot(box, two, preferred_element_type=F32)
    high = sums.astype(BF16)
    low = (sums - high.astype(F32)).astype(BF16)
    for k in range(2):
        rows = slice(row + 64 * k, row + 64 * k + 64)
        for tap in range(9):
            block = (slice(64 * tap, 64 * tap + 64), slice(128 * k, 128 * k + 128))
            columns = slice(128 * tap, 128 * tap + 128)
            high_ref[rows, columns] = high[block]
            low_ref[rows, columns] = low[block]


def most(value):
    return jnp.max(jnp.abs(value).reshape(-1, 8, 128), axis=0)


def edge_kernel(
    count, latent_in, g_in, previous_out, inner_out, outer_out, sems,
):
    core = lax.axis_index("tile") % 2
    inner, outer = 224 * (1 - core), 224 * core
    copies = [
        pltpu.make_async_copy(source, target, sems.at[k])
        for k, (source, target) in enumerate(
            (
                (latent_in.at[pl.ds(count[0] - 2, 2)], previous_out),
                (g_in.at[:, pl.ds(pl.multiple_of(inner, 32), 32)], inner_out),
                (g_in.at[:, pl.ds(pl.multiple_of(outer, 32), 32)], outer_out),
            )
        )
    ]
    for copy in copies:
        copy.start()
    for copy in copies:
        copy.wait()


def weight_kernel(
    count, x_ref, g_ref, box_ref, previous_ref, inner_ref, outer_ref,
    own_ref, sent_ref, high_ref, low_ref, later_ref,
    frames, terms,
):
    used = count[0]
    core, first, second = position()
    frames[:, 0:256] = g_ref[...]
    frames[:, pl.ds(pl.multiple_of(288 - 32 * core, 32), 32)] = inner_ref[...]
    frames[:, pl.ds(pl.multiple_of(256 + 32 * core, 32), 32)] = outer_ref[...]
    for t in range(2, 8):

        @pl.when(t >= used)
        def _():
            frames[t] = jnp.zeros((320, 128), BF16)

    later_ref[...] = frames[0:2]
    for pair in range(4):
        box_sums(
            box_ref[...], frames[2 * pair], frames[2 * pair + 1], high_ref, low_ref, 128 * pair
        )
    peak = [jnp.zeros((8, 128), F32)] * 2
    for dt in range(3):
        parts = [previous_ref[64 * dt :]] if dt < 2 else []
        parts.append(x_ref[: 384 + 64 * dt])
        x = jnp.concatenate(parts, axis=0).T
        for at in range(0, 1152, 256):
            columns = slice(at, min(at + 256, 1152))
            term = jnp.dot(x, high_ref[:, columns], preferred_element_type=F32)
            term = term + jnp.dot(x, low_ref[:, columns], preferred_element_type=F32)
            for k in range(0, term.shape[1], 128):
                tap = 9 * dt + (at + k) // 128
                block = term[:, k : k + 128]
                terms[256 * tap : 256 * tap + 256] = block
                if tap <= 13:
                    peak[0] = jnp.maximum(peak[0], most(block[: 128 if tap == 13 else 256]))
                if tap >= 13:
                    peak[1] = jnp.maximum(peak[1], most(block[128 if tap == 13 else 0 :]))
    for target, half, outer, inner in (
        (own_ref, core, first, second),
        (sent_ref, 1 - core, second, first),
    ):
        for j in range(16):
            start = 3456 * half + 864 * ((j // 4) ^ outer) + 216 * ((j % 4) ^ inner)
            rows = terms[pl.ds(pl.multiple_of(start, 8), 216)]
            target[216 * j : 216 * j + 216] = rows
    low_half = jnp.broadcast_to(jnp.max(peak[0]), (8, 128))
    high_half = jnp.broadcast_to(jnp.max(peak[1]), (8, 128))
    own_ref[3456:3464] = jnp.where(core == 0, low_half, high_half)
    sent_ref[3456:3464] = jnp.where(core == 0, high_half, low_half)


def times_taps(high, low, weight_ref, dt):
    total = None
    for at in range(0, 9, 2):
        taps = range(at, min(at + 2, 9))
        weight = jnp.concatenate([weight_ref[9 * dt + tap] for tap in taps], axis=1)
        columns = slice(128 * at, 128 * at + 128 * len(taps))
        for part in (high, low):
            term = lax.dot_general(
                part[:, columns], weight, (((1,), (1,)), ((), ())), preferred_element_type=F32
            )
            total = term if total is None else total + term
    return total


def input_kernel(
    count, weight_ref, box_ref, later_ref, high_ref, low_ref,
    grad_ref, later_high, later_low, total,
):
    used = count[0]
    for dt in (2, 1, 0):
        start = 64 * (2 - dt)
        term = times_taps(high_ref[start:512], low_ref[start:512], weight_ref, dt)
        if start:
            total[0 : 512 - start] += term
        else:
            total[...] = term
    box_sums(box_ref[...], later_ref[0], later_ref[1], later_high, later_low, 0)
    two = pl.ds(pl.multiple_of(64 * used - 128, 64), 128)
    total[two] += times_taps(later_high[...], later_low[...], weight_ref, 0)
    one = pl.ds(pl.multiple_of(64 * used - 64, 64), 64)
    total[one] += times_taps(later_high[0:64], later_low[0:64], weight_ref, 1)
    slot = lax.broadcasted_iota(jnp.int32, (512, 256), 0) // 64
    grad_ref[...] = jnp.where(slot < used, total[...], F32(0)).astype(BF16)


def shards(activations, grad_output, conv_weight, frame_counts):
    latent = activations.reshape(8, 64, 256)
    cotangent = grad_output.reshape(8, 256, 128)
    box = jnp.asarray(box_matrix(), BF16)
    far = pl.BlockSpec(memory_space=pltpu.HBM)
    near = pl.BlockSpec(memory_space=pltpu.VMEM)
    scalars = pl.BlockSpec(memory_space=pltpu.SMEM)
    params = pltpu.CompilerParams(vmem_limit_bytes=24 * 2**20)
    dma = pltpu.SemaphoreType.DMA
    with jax.named_scope("edges"):
        previous, inner, outer = pl.pallas_call(
            edge_kernel,
            out_shape=(
                jax.ShapeDtypeStruct((2, 64, 256), BF16),
                jax.ShapeDtypeStruct((8, 32, 128), BF16),
                jax.ShapeDtypeStruct((8, 32, 128), BF16),
            ),
            in_specs=[scalars] + [far] * 2,
            out_specs=(near,) * 3,
            scratch_shapes=[dma((3,))],
            compiler_params=pltpu.CompilerParams(vmem_limit_bytes=24 * 2**20),
        )(frame_counts, latent, cotangent)
        previous = shifted(previous, 1, 0).reshape(128, 256)
        inner = swapped(inner, "core")
        outer = swapped(outer, "strip")
    with jax.named_scope("weight_terms"):
        own, sent, high, low, later = pl.pallas_call(
            weight_kernel,
            out_shape=(
                jax.ShapeDtypeStruct((3464, 128), F32),
                jax.ShapeDtypeStruct((3464, 128), F32),
                jax.ShapeDtypeStruct((512, 1152), BF16),
                jax.ShapeDtypeStruct((512, 1152), BF16),
                jax.ShapeDtypeStruct((2, 320, 128), BF16),
            ),
            in_specs=[scalars] + [near] * 6,
            out_specs=(near,) * 5,
            scratch_shapes=[
                pltpu.VMEM((8, 320, 128), BF16),
                pltpu.VMEM((6912, 128), F32),
            ],
            compiler_params=params,
            cost_estimate=pl.CostEstimate(
                flops=3 * 10**9, bytes_accessed=10**7, transcendentals=0
            ),
        )(frame_counts, latent.reshape(512, 256), cotangent, box, previous, inner, outer)
    with jax.named_scope("halves"):
        later = shifted(later, -1, 0)
        received = swapped(sent, "core")
    with jax.named_scope("input_terms"):
        grad_input = pl.pallas_call(
            input_kernel,
            out_shape=jax.ShapeDtypeStruct((512, 256), BF16),
            in_specs=[scalars] + [near] * 5,
            out_specs=near,
            scratch_shapes=[
                pltpu.VMEM((128, 1152), BF16),
                pltpu.VMEM((128, 1152), BF16),
                pltpu.VMEM((512, 256), F32),
            ],
            compiler_params=params,
            cost_estimate=pl.CostEstimate(
                flops=2 * 10**9, bytes_accessed=5 * 10**6, transcendentals=0
            ),
        )(frame_counts, conv_weight, box, later, high, low)
    with jax.named_scope("weight_sum"):
        factor = 1.0 / math.sqrt(16 * 16 * 2048)
        grad_weight, grad_input = summed_everywhere(own, received, grad_input, factor)
    return grad_input.reshape(8, 4, 16, 256), grad_weight.reshape(27, 256, 128)


def solution(mesh):
    placed = (P("tm", "tile", None, None), P("tm", "tile", None, None), P(), P("tm"))
    return jax.shard_map(
        shards,
        mesh=mesh,
        in_specs=placed,
        out_specs=(P("tm", "tile", None, None), P()),
        check_vma=False,
    )
```

```python
import math

import jax
import jax.numpy as jnp
from jax import lax
from jax.experimental import pallas as pl
from jax.experimental.pallas import tpu as pltpu
from jax.sharding import PartitionSpec as P

BOTH = ("tm", "tile")
F32 = jnp.float32
BF16 = jnp.bfloat16
F16 = jnp.float16


def moved(rank, kind, step):
    tm, tile = divmod(rank, 16)
    y, x = divmod(tm, 4)
    z, core = divmod(tile, 2)
    half = core ^ ((x + y + z) & 1)
    if kind == "strip":
        tile += 1 if core else -1
        return tm * 16 + tile if 0 <= tile < 16 else None
    if kind == "core":
        half ^= 1
    elif kind == "pair":
        z ^= 1
    elif kind == "z":
        z = (z + step if z % 2 else z - step) % 8
    elif (kind == "first") == (half == 0):
        x ^= step
    else:
        y ^= step
    return (y * 4 + x) * 16 + z * 2 + (half ^ ((x + y + z) & 1))


def swapped(value, kind, step=1):
    pairs = [(rank, moved(rank, kind, step)) for rank in range(256)]
    return lax.ppermute(value, BOTH, [pair for pair in pairs if pair[1] is not None])


def shifted(value, tm_step, tile_step):
    pairs = []
    for rank in range(256):
        tm, tile = divmod(rank, 16)
        tm, tile = tm + tm_step, tile + tile_step
        if 0 <= tm < 16 and 0 <= tile < 16:
            pairs.append((rank, tm * 16 + tile))
    return lax.ppermute(value, BOTH, pairs)


def position():
    tm, tile = lax.axis_index("tm"), lax.axis_index("tile")
    y, x, z, core = tm // 4, tm % 4, tile // 2, tile % 2
    half = core ^ ((x + y + z) & 1)
    return half, jnp.where(half == 0, x, y), jnp.where(half == 0, y, x)


def power(exponent):
    whole = exponent.astype(jnp.int32)
    size = jnp.abs(whole)
    result = jnp.ones_like(exponent)
    for bit in range(7):
        factor = jnp.where(whole >= 0, F32(2.0 ** (2**bit)), F32(2.0 ** -(2**bit)))
        result = result * jnp.where((size >> bit) & 1 == 1, factor, F32(1))
    return lax.optimization_barrier(result)


def packed(value, exponent, scale):
    tail = jnp.broadcast_to(exponent.astype(F16), (8, 128))
    return jnp.concatenate([(value * scale).astype(F16), tail], axis=0)


def opened(message):
    exponent = message[-8:-7].astype(F32)
    return message[:-8].astype(F32) * power(-exponent), exponent


def scattered(pieces, exponent, kind, after=None):
    scale = power(exponent)
    lowest = exponent
    parts = [pieces[0]]
    arrived = [swapped(packed(pieces[step], exponent, scale), kind, step) for step in (1, 3, 2)]
    if after is not None:
        *arrived, after = lax.optimization_barrier((*arrived, after))
    for message in arrived:
        part, theirs = opened(message)
        parts.append(part)
        lowest = jnp.minimum(lowest, theirs)
    return (parts[0] + parts[1]) + (parts[2] + parts[3]), lowest - 2, after


def placed_at(buffer, piece, place):
    return lax.dynamic_update_index_in_dim(buffer, piece, place, 0)


def summed_everywhere(own, received, grad_input, factor):
    half, first, second = position()
    bound = own[3456:3457] + received[3456:3457]
    exponent = jnp.floor(13 - jnp.log2(jnp.maximum(bound, F32(1e-30))))
    pieces = [own[r : r + 864] + received[r : r + 864] for r in range(0, 3456, 864)]
    total, exponent, grad_input = scattered(pieces, exponent, "first", grad_input)
    pieces = [total[r : r + 216] for r in range(0, 864, 216)]
    total, exponent, _ = scattered(pieces, exponent, "second")
    message = packed(total, exponent, power(exponent))
    (a, e), (b, f) = opened(message), opened(swapped(message, "pair"))
    total, exponent = a + b, jnp.minimum(e, f) - 1
    message = packed(total, exponent, power(exponent))
    parts = [opened(message)] + [opened(swapped(message, "z", step)) for step in (3, 2, 1)]
    total = (parts[0][0] + parts[1][0]) + (parts[2][0] + parts[3][0])
    exponent = jnp.stack([part[1] for part in parts]).min(axis=0) - 2
    message = packed(total, exponent, power(exponent))
    row = jnp.zeros((4, 224, 128), F16)
    for step in (0, 1, 3, 2):
        theirs = swapped(message, "second", step) if step else message
        row = placed_at(row, theirs, second ^ step)
    pieces = [row] + [swapped(row, "first", step) for step in (1, 3, 2)]
    mine = theirs = jnp.zeros((4, 4, 224, 128), F16)
    for pair, steps in ((pieces[:2], (0, 1)), (pieces[2:], (3, 2))):
        other = swapped(jnp.stack(pair), "core")
        for k, step in enumerate(steps):
            mine = placed_at(mine, pair[k], first ^ step)
            theirs = placed_at(theirs, other[k], second ^ step)
    result = jnp.zeros((2, 4, 4, 216, 128), F32)
    for at, pieces in ((half, mine), (1 - half, theirs)):
        scale = power(-pieces[:, :, -8:-7].astype(F32)) * F32(factor)
        result = placed_at(result, pieces[:, :, :-8].astype(F32) * scale, at)
    return result, grad_input


def box_matrix(box_ref):
    j = lax.broadcasted_iota(jnp.int32, (16, 320), 0)
    column = lax.broadcasted_iota(jnp.int32, (16, 320), 1)
    w = column % 32
    h = jnp.where(column < 256, column // 32, jnp.where(column < 288, -1, 8))
    for dw in range(3):
        from_first = w - (2 * j + 1 - dw)
        inside = (from_first == 0) | (from_first == 1)
        for dh in range(3):
            for i in range(4):
                from_top = h - (2 * i + 1 - dh)
                ones = inside & ((from_top == 0) | (from_top == 1))
                row = 64 * (3 * dh + dw) + 16 * i
                box_ref[row : row + 16] = jnp.where(ones, F32(1), F32(0)).astype(BF16)


def box_sums(box, frame, next_frame, high_ref, low_ref, row):
    two = jnp.concatenate([frame, next_frame], axis=1)
    sums = jnp.dot(box, two, preferred_element_type=F32)
    high = sums.astype(BF16)
    low = (sums - high.astype(F32)).astype(BF16)
    for k in range(2):
        rows = slice(row + 64 * k, row + 64 * k + 64)
        for tap in range(9):
            block = (slice(64 * tap, 64 * tap + 64), slice(128 * k, 128 * k + 128))
            columns = slice(128 * tap, 128 * tap + 128)
            high_ref[rows, columns] = high[block]
            low_ref[rows, columns] = low[block]


def most(value):
    return jnp.max(jnp.abs(value).reshape(-1, 8, 128), axis=0)


def edge_kernel(
    count, latent_in, g_in, previous_out, inner_out, outer_out, sems,
):
    core = lax.axis_index("tile") % 2
    inner, outer = 224 * (1 - core), 224 * core
    copies = [
        pltpu.make_async_copy(source, target, sems.at[k])
        for k, (source, target) in enumerate(
            (
                (latent_in.at[pl.ds(count[0] - 2, 2)], previous_out),
                (g_in.at[:, pl.ds(pl.multiple_of(inner, 32), 32)], inner_out),
                (g_in.at[:, pl.ds(pl.multiple_of(outer, 32), 32)], outer_out),
            )
        )
    ]
    for copy in copies:
        copy.start()
    for copy in copies:
        copy.wait()


def weight_kernel(
    count, x_ref, g_ref, previous_ref, inner_ref, outer_ref,
    own_ref, sent_ref, high_ref, low_ref, later_ref, box_ref,
    frames, terms,
):
    used = count[0]
    core = lax.axis_index("tile") % 2
    half, first, second = position()
    box_matrix(box_ref)
    frames[:, 0:256] = g_ref[...]
    frames[:, pl.ds(pl.multiple_of(288 - 32 * core, 32), 32)] = inner_ref[...]
    frames[:, pl.ds(pl.multiple_of(256 + 32 * core, 32), 32)] = outer_ref[...]
    for t in range(2, 8):

        @pl.when(t >= used)
        def _():
            frames[t] = jnp.zeros((320, 128), BF16)

    later_ref[...] = frames[0:2]
    for pair in range(4):
        box_sums(
            box_ref[...], frames[2 * pair], frames[2 * pair + 1], high_ref, low_ref, 128 * pair
        )
    peak = [jnp.zeros((8, 128), F32)] * 2
    for dt in range(3):
        parts = [previous_ref[64 * dt :]] if dt < 2 else []
        parts.append(x_ref[: 384 + 64 * dt])
        x = jnp.concatenate(parts, axis=0).T
        for at in range(0, 1152, 256):
            columns = slice(at, min(at + 256, 1152))
            term = jnp.dot(x, high_ref[:, columns], preferred_element_type=F32)
            term = term + jnp.dot(x, low_ref[:, columns], preferred_element_type=F32)
            for k in range(0, term.shape[1], 128):
                tap = 9 * dt + (at + k) // 128
                block = term[:, k : k + 128]
                terms[256 * tap : 256 * tap + 256] = block
                if tap <= 13:
                    peak[0] = jnp.maximum(peak[0], most(block[: 128 if tap == 13 else 256]))
                if tap >= 13:
                    peak[1] = jnp.maximum(peak[1], most(block[128 if tap == 13 else 0 :]))
    for target, which, outer, inner in (
        (own_ref, half, first, second),
        (sent_ref, 1 - half, second, first),
    ):
        for j in range(16):
            start = 3456 * which + 864 * ((j // 4) ^ outer) + 216 * ((j % 4) ^ inner)
            rows = terms[pl.ds(pl.multiple_of(start, 8), 216)]
            target[216 * j : 216 * j + 216] = rows
    low_half = jnp.broadcast_to(jnp.max(peak[0]), (8, 128))
    high_half = jnp.broadcast_to(jnp.max(peak[1]), (8, 128))
    own_ref[3456:3464] = jnp.where(half == 0, low_half, high_half)
    sent_ref[3456:3464] = jnp.where(half == 0, high_half, low_half)


def times_taps(high, low, weight_ref, dt):
    total = None
    for at in range(0, 9, 2):
        taps = range(at, min(at + 2, 9))
        weight = jnp.concatenate([weight_ref[9 * dt + tap] for tap in taps], axis=1)
        columns = slice(128 * at, 128 * at + 128 * len(taps))
        for part in (high, low):
            term = lax.dot_general(
                part[:, columns], weight, (((1,), (1,)), ((), ())), preferred_element_type=F32
            )
            total = term if total is None else total + term
    return total


def input_kernel(
    count, weight_ref, box_ref, later_ref, high_ref, low_ref,
    grad_ref, later_high, later_low, total,
):
    used = count[0]
    for dt in (2, 1, 0):
        start = 64 * (2 - dt)
        term = times_taps(high_ref[start:512], low_ref[start:512], weight_ref, dt)
        if start:
            total[0 : 512 - start] += term
        else:
            total[...] = term
    box_sums(box_ref[...], later_ref[0], later_ref[1], later_high, later_low, 0)
    two = pl.ds(pl.multiple_of(64 * used - 128, 64), 128)
    total[two] += times_taps(later_high[...], later_low[...], weight_ref, 0)
    one = pl.ds(pl.multiple_of(64 * used - 64, 64), 64)
    total[one] += times_taps(later_high[0:64], later_low[0:64], weight_ref, 1)
    slot = lax.broadcasted_iota(jnp.int32, (512, 256), 0) // 64
    grad_ref[...] = jnp.where(slot < used, total[...], F32(0)).astype(BF16)


def shards(activations, grad_output, conv_weight, frame_counts):
    latent = activations.reshape(8, 64, 256)
    cotangent = grad_output.reshape(8, 256, 128)
    far = pl.BlockSpec(memory_space=pltpu.HBM)
    near = pl.BlockSpec(memory_space=pltpu.VMEM)
    scalars = pl.BlockSpec(memory_space=pltpu.SMEM)
    params = pltpu.CompilerParams(vmem_limit_bytes=24 * 2**20)
    dma = pltpu.SemaphoreType.DMA
    with jax.named_scope("edges"):
        previous, inner, outer = pl.pallas_call(
            edge_kernel,
            out_shape=(
                jax.ShapeDtypeStruct((2, 64, 256), BF16),
                jax.ShapeDtypeStruct((8, 32, 128), BF16),
                jax.ShapeDtypeStruct((8, 32, 128), BF16),
            ),
            in_specs=[scalars] + [far] * 2,
            out_specs=(near,) * 3,
            scratch_shapes=[dma((3,))],
            compiler_params=pltpu.CompilerParams(vmem_limit_bytes=24 * 2**20),
        )(frame_counts, latent, cotangent)
        previous = shifted(previous, 1, 0).reshape(128, 256)
        inner = swapped(inner, "core")
        outer = swapped(outer, "strip")
    with jax.named_scope("weight_terms"):
        own, sent, high, low, later, box = pl.pallas_call(
            weight_kernel,
            out_shape=(
                jax.ShapeDtypeStruct((3464, 128), F32),
                jax.ShapeDtypeStruct((3464, 128), F32),
                jax.ShapeDtypeStruct((512, 1152), BF16),
                jax.ShapeDtypeStruct((512, 1152), BF16),
                jax.ShapeDtypeStruct((2, 320, 128), BF16),
                jax.ShapeDtypeStruct((576, 320), BF16),
            ),
            in_specs=[scalars] + [near] * 5,
            out_specs=(near,) * 6,
            scratch_shapes=[
                pltpu.VMEM((8, 320, 128), BF16),
                pltpu.VMEM((6912, 128), F32),
            ],
            compiler_params=params,
            cost_estimate=pl.CostEstimate(
                flops=3 * 10**9, bytes_accessed=10**7, transcendentals=0
            ),
        )(frame_counts, latent.reshape(512, 256), cotangent, previous, inner, outer)
    with jax.named_scope("halves"):
        later = shifted(later, -1, 0)
        received = swapped(sent, "core")
    with jax.named_scope("input_terms"):
        grad_input = pl.pallas_call(
            input_kernel,
            out_shape=jax.ShapeDtypeStruct((512, 256), BF16),
            in_specs=[scalars] + [near] * 5,
            out_specs=near,
            scratch_shapes=[
                pltpu.VMEM((128, 1152), BF16),
                pltpu.VMEM((128, 1152), BF16),
                pltpu.VMEM((512, 256), F32),
            ],
            compiler_params=params,
            cost_estimate=pl.CostEstimate(
                flops=2 * 10**9, bytes_accessed=5 * 10**6, transcendentals=0
            ),
        )(frame_counts, conv_weight, box, later, high, low)
    with jax.named_scope("weight_sum"):
        factor = 1.0 / math.sqrt(16 * 16 * 2048)
        grad_weight, grad_input = summed_everywhere(own, received, grad_input, factor)
    return grad_input.reshape(8, 4, 16, 256), grad_weight.reshape(27, 256, 128)


def solution(mesh):
    placed = (P("tm", "tile", None, None), P("tm", "tile", None, None), P(), P("tm"))
    return jax.shard_map(
        shards,
        mesh=mesh,
        in_specs=placed,
        out_specs=(P("tm", "tile", None, None), P()),
        check_vma=False,
    )
```

```python
import functools
import math

import jax
import jax.numpy as jnp
from jax import lax
from jax.experimental import pallas as pl
from jax.experimental.pallas import tpu as pltpu
from jax.sharding import PartitionSpec as P

BOTH = ("tm", "tile")
ORDER = (0, 1, 3, 2)
F32 = jnp.float32
BF16 = jnp.bfloat16
F16 = jnp.float16


def moved(rank, kind, step):
    tm, tile = divmod(rank, 16)
    y, x = divmod(tm, 4)
    z, core = divmod(tile, 2)
    half = core ^ ((x + y + z) & 1)
    if kind == "strip":
        tile += 1 if core else -1
        return tm * 16 + tile if 0 <= tile < 16 else None
    if kind == "core":
        half ^= 1
    elif kind == "pair":
        z ^= 1
    elif kind == "z":
        z = (z + step if z % 2 else z - step) % 8
    elif (kind == "first") == (half == 0):
        x ^= step
    else:
        y ^= step
    return (y * 4 + x) * 16 + z * 2 + (half ^ ((x + y + z) & 1))


def swapped(value, kind, step=1):
    pairs = [(rank, moved(rank, kind, step)) for rank in range(256)]
    return lax.ppermute(value, BOTH, [pair for pair in pairs if pair[1] is not None])


def shifted(value, tm_step, tile_step):
    pairs = []
    for rank in range(256):
        tm, tile = divmod(rank, 16)
        tm, tile = tm + tm_step, tile + tile_step
        if 0 <= tm < 16 and 0 <= tile < 16:
            pairs.append((rank, tm * 16 + tile))
    return lax.ppermute(value, BOTH, pairs)


def position():
    tm, tile = lax.axis_index("tm"), lax.axis_index("tile")
    y, x, z, core = tm // 4, tm % 4, tile // 2, tile % 2
    half = core ^ ((x + y + z) & 1)
    return half, jnp.where(half == 0, x, y), jnp.where(half == 0, y, x)


def power(exponent):
    whole = exponent.astype(jnp.int32)
    size = jnp.abs(whole)
    result = jnp.ones_like(exponent)
    for bit in range(7):
        factor = jnp.where(whole >= 0, F32(2.0 ** (2**bit)), F32(2.0 ** -(2**bit)))
        result = result * jnp.where((size >> bit) & 1 == 1, factor, F32(1))
    return lax.optimization_barrier(result)


def packed(value, exponent, scale):
    tail = jnp.broadcast_to(exponent.astype(F16), (8, 128))
    return jnp.concatenate([(value * scale).astype(F16), tail], axis=0)


def fitting(bound):
    return jnp.floor(13 - jnp.log2(jnp.maximum(bound, F32(1e-30))))


def opened(message):
    exponent = message[-8:-7].astype(F32)
    return message[:-8].astype(F32) * power(-exponent), exponent


def scattered(pieces, exponent, kind, after=None):
    scale = power(exponent)
    lowest = exponent
    parts = [pieces[0]]
    arrived = [swapped(packed(pieces[step], exponent, scale), kind, step) for step in ORDER[1:]]
    if after is not None:
        *arrived, after = lax.optimization_barrier((*arrived, after))
    for message in arrived:
        part, theirs = opened(message)
        parts.append(part)
        lowest = jnp.minimum(lowest, theirs)
    return (parts[0] + parts[1]) + (parts[2] + parts[3]), lowest - 2, after


def placed_at(buffer, piece, place):
    return lax.dynamic_update_index_in_dim(buffer, piece, place, 0)


def summed_everywhere(own, received, partial, finished, factor):
    half, first, second = position()
    received, theirs = opened(received)
    exponent = fitting(own[3456:3457] + 2.0**14 * power(-theirs))
    pieces = [own[r : r + 864] + received[r : r + 864] for r in range(0, 3456, 864)]
    total, exponent, partial = scattered(pieces, exponent, "first", partial)
    pieces = [total[r : r + 216] for r in range(0, 864, 216)]
    total, exponent, grad_input = scattered(pieces, exponent, "second", finished(partial))
    message = packed(total, exponent, power(exponent))
    (a, e), (b, f) = opened(message), opened(swapped(message, "pair"))
    total, exponent = a + b, jnp.minimum(e, f) - 1
    message = packed(total, exponent, power(exponent))
    parts = [opened(message)] + [opened(swapped(message, "z", step)) for step in (1, 2, 3)]
    total = (parts[0][0] + parts[3][0]) + (parts[1][0] + parts[2][0])
    exponent = jnp.stack([part[1] for part in parts]).min(axis=0) - 2
    message = packed(total, exponent, power(exponent))
    row = jnp.zeros((4, 224, 128), F16)
    for step in ORDER:
        theirs = swapped(message, "second", step) if step else message
        row = placed_at(row, theirs, second ^ step)
    mine = [row] + [swapped(row, "first", step) for step in ORDER[1:]]
    theirs = [
        piece for pair in (mine[:2], mine[2:]) for piece in swapped(jnp.stack(pair), "core")
    ]

    def restored(piece):
        scale = power(-piece[:, -8:-7].astype(F32)) * F32(factor)
        return piece[:, :-8].astype(F32) * scale

    result = stored([restored(piece) for piece in mine])
    result = stored([restored(piece) for piece in theirs], result)
    return result, grad_input


def box_matrix(box_ref):
    j = lax.broadcasted_iota(jnp.int32, (16, 320), 0)
    column = lax.broadcasted_iota(jnp.int32, (16, 320), 1)
    w = column % 32
    h = jnp.where(column < 256, column // 32, jnp.where(column < 288, -1, 8))
    for dw in range(3):
        from_first = w - (2 * j + 1 - dw)
        inside = (from_first == 0) | (from_first == 1)
        for dh in range(3):
            for i in range(4):
                from_top = h - (2 * i + 1 - dh)
                ones = inside & ((from_top == 0) | (from_top == 1))
                row = 64 * (3 * dh + dw) + 16 * i
                box_ref[row : row + 16] = jnp.where(ones, F32(1), F32(0)).astype(BF16)


def box_sums(box, frame, next_frame, high_ref, low_ref, row):
    two = jnp.concatenate([frame, next_frame], axis=1)
    sums = jnp.dot(box, two, preferred_element_type=F32)
    high = sums.astype(BF16)
    low = (sums - high.astype(F32)).astype(BF16)
    for k in range(2):
        rows = slice(row + 64 * k, row + 64 * k + 64)
        for tap in range(9):
            block = (slice(64 * tap, 64 * tap + 64), slice(128 * k, 128 * k + 128))
            columns = slice(128 * tap, 128 * tap + 128)
            high_ref[rows, columns] = high[block]
            low_ref[rows, columns] = low[block]


def most(value):
    return jnp.max(jnp.abs(value).reshape(-1, 8, 128), axis=0)


def edge_kernel(
    count, latent_in, g_in, previous_out, inner_out, outer_out, sems,
):
    core = lax.axis_index("tile") % 2
    inner, outer = 224 * (1 - core), 224 * core
    copies = [
        pltpu.make_async_copy(source, target, sems.at[k])
        for k, (source, target) in enumerate(
            (
                (latent_in.at[pl.ds(count[0] - 2, 2)], previous_out),
                (g_in.at[:, pl.ds(pl.multiple_of(inner, 32), 32)], inner_out),
                (g_in.at[:, pl.ds(pl.multiple_of(outer, 32), 32)], outer_out),
            )
        )
    ]
    for copy in copies:
        copy.start()
    for copy in copies:
        copy.wait()


def weight_kernel(
    count, x_ref, g_ref, previous_ref, inner_ref, outer_ref,
    own_ref, sent_ref, high_ref, low_ref, later_ref, box_ref,
    frames, terms,
):
    used = count[0]
    core = lax.axis_index("tile") % 2
    half, first, second = position()
    box_matrix(box_ref)
    frames[:, 0:256] = g_ref[...]
    frames[:, pl.ds(pl.multiple_of(288 - 32 * core, 32), 32)] = inner_ref[...]
    frames[:, pl.ds(pl.multiple_of(256 + 32 * core, 32), 32)] = outer_ref[...]
    for t in range(2, 8):

        @pl.when(t >= used)
        def _():
            frames[t] = jnp.zeros((320, 128), BF16)

    later_ref[...] = frames[0:2]
    for pair in range(4):
        box_sums(
            box_ref[...], frames[2 * pair], frames[2 * pair + 1], high_ref, low_ref, 128 * pair
        )
    peak = [jnp.zeros((8, 128), F32)] * 2
    for dt in range(3):
        parts = [previous_ref[64 * dt :]] if dt < 2 else []
        parts.append(x_ref[: 384 + 64 * dt])
        x = jnp.concatenate(parts, axis=0).T
        for at in range(0, 1152, 256):
            columns = slice(at, min(at + 256, 1152))
            term = jnp.dot(x, high_ref[:, columns], preferred_element_type=F32)
            term = term + jnp.dot(x, low_ref[:, columns], preferred_element_type=F32)
            for k in range(0, term.shape[1], 128):
                tap = 9 * dt + (at + k) // 128
                block = term[:, k : k + 128]
                terms[256 * tap : 256 * tap + 256] = block
                if tap <= 13:
                    peak[0] = jnp.maximum(peak[0], most(block[: 128 if tap == 13 else 256]))
                if tap >= 13:
                    peak[1] = jnp.maximum(peak[1], most(block[128 if tap == 13 else 0 :]))
    for target, which, outer, inner in (
        (own_ref, half, first, second),
        (sent_ref, 1 - half, second, first),
    ):
        for j in range(16):
            start = 3456 * which + 864 * ((j // 4) ^ outer) + 216 * ((j % 4) ^ inner)
            rows = terms[pl.ds(pl.multiple_of(start, 8), 216)]
            target[216 * j : 216 * j + 216] = rows
    low_half = jnp.broadcast_to(jnp.max(peak[0]), (8, 128))
    high_half = jnp.broadcast_to(jnp.max(peak[1]), (8, 128))
    own_ref[3456:3464] = jnp.where(half == 0, low_half, high_half)
    sent_ref[3456:3464] = jnp.where(half == 0, high_half, low_half)


def times_taps(high, low, weight_ref, dt):
    total = None
    for at in range(0, 9, 2):
        taps = range(at, min(at + 2, 9))
        weight = jnp.concatenate([weight_ref[9 * dt + tap] for tap in taps], axis=1)
        columns = slice(128 * at, 128 * at + 128 * len(taps))
        for part in (high, low):
            term = lax.dot_general(
                part[:, columns], weight, (((1,), (1,)), ((), ())), preferred_element_type=F32
            )
            total = term if total is None else total + term
    return total


def input_kernel(weight_ref, high_ref, low_ref, total):
    for dt in (2, 1, 0):
        start = 64 * (2 - dt)
        term = times_taps(high_ref[start:512], low_ref[start:512], weight_ref, dt)
        if start:
            total[0 : 512 - start] += term
        else:
            total[...] = term


def later_kernel(
    count, weight_ref, box_ref, later_ref, before_ref, grad_ref, later_high, later_low, total
):
    used = count[0]
    total[...] = before_ref[...]
    box_sums(box_ref[...], later_ref[0], later_ref[1], later_high, later_low, 0)
    two = pl.ds(pl.multiple_of(64 * used - 128, 64), 128)
    total[two] += times_taps(later_high[...], later_low[...], weight_ref, 0)
    one = pl.ds(pl.multiple_of(64 * used - 64, 64), 64)
    total[one] += times_taps(later_high[0:64], later_low[0:64], weight_ref, 1)
    slot = lax.broadcasted_iota(jnp.int32, (512, 256), 0) // 64
    grad_ref[...] = jnp.where(slot < used, total[...], F32(0)).astype(BF16)


def store_kernel(other, *refs):
    pieces, (out, sems) = refs[:4], refs[-2:]
    half, first, second = position()
    half, place = (1 - half, second) if other else (half, first)
    copies = [
        pltpu.make_async_copy(piece, out.at[half, place ^ step], sems.at[step])
        for step, piece in zip(ORDER, pieces)
    ]
    for copy in copies:
        copy.start()
    for copy in copies:
        copy.wait()


def stored(pieces, before=None):
    far = pl.BlockSpec(memory_space=pltpu.HBM)
    near = pl.BlockSpec(memory_space=pltpu.VMEM)
    other = before is not None
    return pl.pallas_call(
        functools.partial(store_kernel, other),
        out_shape=jax.ShapeDtypeStruct((2, 4, 4, 216, 128), F32),
        in_specs=[near] * 4 + [far] * other,
        out_specs=far,
        scratch_shapes=[pltpu.SemaphoreType.DMA((4,))],
        input_output_aliases={4: 0} if other else {},
        compiler_params=pltpu.CompilerParams(vmem_limit_bytes=24 * 2**20),
        cost_estimate=pl.CostEstimate(flops=0, bytes_accessed=4 * 10**6, transcendentals=0),
    )(*pieces, *([before] if other else []))


def shards(activations, grad_output, conv_weight, frame_counts):
    latent = activations.reshape(8, 64, 256)
    cotangent = grad_output.reshape(8, 256, 128)
    far = pl.BlockSpec(memory_space=pltpu.HBM)
    near = pl.BlockSpec(memory_space=pltpu.VMEM)
    scalars = pl.BlockSpec(memory_space=pltpu.SMEM)
    params = pltpu.CompilerParams(vmem_limit_bytes=24 * 2**20)
    dma = pltpu.SemaphoreType.DMA
    with jax.named_scope("edges"):
        previous, inner, outer = pl.pallas_call(
            edge_kernel,
            out_shape=(
                jax.ShapeDtypeStruct((2, 64, 256), BF16),
                jax.ShapeDtypeStruct((8, 32, 128), BF16),
                jax.ShapeDtypeStruct((8, 32, 128), BF16),
            ),
            in_specs=[scalars] + [far] * 2,
            out_specs=(near,) * 3,
            scratch_shapes=[dma((3,))],
            compiler_params=pltpu.CompilerParams(vmem_limit_bytes=24 * 2**20),
        )(frame_counts, latent, cotangent)
        previous = shifted(previous, 1, 0).reshape(128, 256)
        inner = swapped(inner, "core")
        outer = swapped(outer, "strip")
    with jax.named_scope("weight_terms"):
        own, sent, high, low, later, box = pl.pallas_call(
            weight_kernel,
            out_shape=(
                jax.ShapeDtypeStruct((3464, 128), F32),
                jax.ShapeDtypeStruct((3464, 128), F32),
                jax.ShapeDtypeStruct((512, 1152), BF16),
                jax.ShapeDtypeStruct((512, 1152), BF16),
                jax.ShapeDtypeStruct((2, 320, 128), BF16),
                jax.ShapeDtypeStruct((576, 320), BF16),
            ),
            in_specs=[scalars] + [near] * 5,
            out_specs=(near,) * 6,
            scratch_shapes=[
                pltpu.VMEM((8, 320, 128), BF16),
                pltpu.VMEM((6912, 128), F32),
            ],
            compiler_params=params,
            cost_estimate=pl.CostEstimate(
                flops=3 * 10**9, bytes_accessed=10**7, transcendentals=0
            ),
        )(frame_counts, latent.reshape(512, 256), cotangent, previous, inner, outer)
    with jax.named_scope("halves"):
        exponent = fitting(sent[3456:3457])
        received = swapped(packed(sent[:3456], exponent, power(exponent)), "core")
        later = shifted(later, -1, 0)
    with jax.named_scope("input_terms"):
        partial = pl.pallas_call(
            input_kernel,
            out_shape=jax.ShapeDtypeStruct((512, 256), F32),
            in_specs=[near] * 3,
            out_specs=near,
            compiler_params=params,
            cost_estimate=pl.CostEstimate(
                flops=2 * 10**9, bytes_accessed=5 * 10**6, transcendentals=0
            ),
        )(conv_weight, high, low)
    with jax.named_scope("later"):

        def finished(partial):
            return pl.pallas_call(
                later_kernel,
                out_shape=jax.ShapeDtypeStruct((512, 256), BF16),
                in_specs=[scalars] + [near] * 4,
                out_specs=near,
                scratch_shapes=[
                    pltpu.VMEM((128, 1152), BF16),
                    pltpu.VMEM((128, 1152), BF16),
                    pltpu.VMEM((512, 256), F32),
                ],
                compiler_params=params,
                cost_estimate=pl.CostEstimate(
                    flops=5 * 10**8, bytes_accessed=10**6, transcendentals=0
                ),
            )(frame_counts, conv_weight, box, later, partial)

    with jax.named_scope("weight_sum"):
        factor = 1.0 / math.sqrt(16 * 16 * 2048)
        grad_weight, grad_input = summed_everywhere(own, received, partial, finished, factor)
    return grad_input.reshape(8, 4, 16, 256), grad_weight.reshape(27, 256, 128)


def solution(mesh):
    placed = (P("tm", "tile", None, None), P("tm", "tile", None, None), P(), P("tm"))
    return jax.shard_map(
        shards,
        mesh=mesh,
        in_specs=placed,
        out_specs=(P("tm", "tile", None, None), P()),
        check_vma=False,
    )
```

```python
import functools
import math

import jax
import jax.numpy as jnp
from jax import lax
from jax.experimental import pallas as pl
from jax.experimental.pallas import tpu as pltpu
from jax.sharding import PartitionSpec as P

BOTH = ("tm", "tile")
ORDER = (0, 1, 3, 2)
F32 = jnp.float32
BF16 = jnp.bfloat16
F16 = jnp.float16


def moved(rank, kind, step):
    tm, tile = divmod(rank, 16)
    y, x = divmod(tm, 4)
    z, core = divmod(tile, 2)
    half = core ^ ((x + y + z) & 1)
    if kind == "strip":
        tile += 1 if core else -1
        return tm * 16 + tile if 0 <= tile < 16 else None
    if kind == "core":
        half ^= 1
    elif kind == "pair":
        z ^= 1
    elif kind == "z":
        z = (z + step if z % 2 else z - step) % 8
    elif (kind == "first") == (half == 0):
        x ^= step
    else:
        y ^= step
    return (y * 4 + x) * 16 + z * 2 + (half ^ ((x + y + z) & 1))


def swapped(value, kind, step=1):
    pairs = [(rank, moved(rank, kind, step)) for rank in range(256)]
    return lax.ppermute(value, BOTH, [pair for pair in pairs if pair[1] is not None])


def shifted(value, tm_step, tile_step):
    pairs = []
    for rank in range(256):
        tm, tile = divmod(rank, 16)
        tm, tile = tm + tm_step, tile + tile_step
        if 0 <= tm < 16 and 0 <= tile < 16:
            pairs.append((rank, tm * 16 + tile))
    return lax.ppermute(value, BOTH, pairs)


def position():
    tm, tile = lax.axis_index("tm"), lax.axis_index("tile")
    y, x, z, core = tm // 4, tm % 4, tile // 2, tile % 2
    half = core ^ ((x + y + z) & 1)
    return half, jnp.where(half == 0, x, y), jnp.where(half == 0, y, x)


def power(exponent):
    whole = exponent.astype(jnp.int32)
    size = jnp.abs(whole)
    result = jnp.ones_like(exponent)
    for bit in range(7):
        factor = jnp.where(whole >= 0, F32(2.0 ** (2**bit)), F32(2.0 ** -(2**bit)))
        result = result * jnp.where((size >> bit) & 1 == 1, factor, F32(1))
    return lax.optimization_barrier(result)


def packed(value, exponent, scale):
    tail = jnp.broadcast_to(exponent.astype(F16), (8, 128))
    return jnp.concatenate([(value * scale).astype(F16), tail], axis=0)


def fitting(bound):
    return jnp.floor(13 - jnp.log2(jnp.maximum(bound, F32(1e-30))))


def opened(message):
    exponent = message[-8:-7].astype(F32)
    return message[:-8].astype(F32) * power(-exponent), exponent


def scattered(pieces, exponent, kind, after=None):
    scale = power(exponent)
    lowest = exponent
    parts = [pieces[0]]
    arrived = [swapped(packed(pieces[step], exponent, scale), kind, step) for step in ORDER[1:]]
    if after is not None:
        *arrived, after = lax.optimization_barrier((*arrived, after))
    for message in arrived:
        part, theirs = opened(message)
        parts.append(part)
        lowest = jnp.minimum(lowest, theirs)
    return (parts[0] + parts[1]) + (parts[2] + parts[3]), lowest - 2, after


def placed_at(buffer, piece, place):
    return lax.dynamic_update_index_in_dim(buffer, piece, place, 0)


def summed_everywhere(own, received, partial, finished, factor):
    half, first, second = position()
    received, theirs = opened(received)
    exponent = fitting(own[3456:3457] + 2.0**14 * power(-theirs))
    pieces = [own[r : r + 864] + received[r : r + 864] for r in range(0, 3456, 864)]
    total, exponent, partial = scattered(pieces, exponent, "first", partial)
    pieces = [total[r : r + 216] for r in range(0, 864, 216)]
    total, exponent, grad_input = scattered(pieces, exponent, "second", finished(partial))
    message = packed(total, exponent, power(exponent))
    (a, e), (b, f) = opened(message), opened(swapped(message, "pair"))
    total, exponent = a + b, jnp.minimum(e, f) - 1
    message = packed(total, exponent, power(exponent))
    parts = [opened(message)] + [opened(swapped(message, "z", step)) for step in (1, 2, 3)]
    total = (parts[0][0] + parts[3][0]) + (parts[1][0] + parts[2][0])
    exponent = jnp.stack([part[1] for part in parts]).min(axis=0) - 2
    message = packed(total, exponent, power(exponent))
    row = jnp.zeros((4, 224, 128), F16)
    for step in ORDER:
        theirs = swapped(message, "second", step) if step else message
        row = placed_at(row, theirs, second ^ step)
    mine = [row] + [swapped(row, "first", step) for step in ORDER[1:]]
    theirs = [
        piece for pair in (mine[:2], mine[2:]) for piece in swapped(jnp.stack(pair), "core")
    ]

    def restored(piece):
        scale = power(-piece[:, -8:-7].astype(F32)) * F32(factor)
        return piece[:, :-8].astype(F32) * scale

    result = stored([restored(piece) for piece in mine])
    result = stored([restored(piece) for piece in theirs], result)
    return result, grad_input


def box_matrix(box_ref):
    j = lax.broadcasted_iota(jnp.int32, (16, 320), 0)
    column = lax.broadcasted_iota(jnp.int32, (16, 320), 1)
    w = column % 32
    h = jnp.where(column < 256, column // 32, jnp.where(column < 288, -1, 8))
    for dw in range(3):
        from_first = w - (2 * j + 1 - dw)
        inside = (from_first == 0) | (from_first == 1)
        for dh in range(3):
            for i in range(4):
                from_top = h - (2 * i + 1 - dh)
                ones = inside & ((from_top == 0) | (from_top == 1))
                row = 64 * (3 * dh + dw) + 16 * i
                box_ref[row : row + 16] = jnp.where(ones, F32(1), F32(0)).astype(BF16)


def box_sums(box, frame, next_frame, high_ref, low_ref, row):
    two = jnp.concatenate([frame, next_frame], axis=1)
    sums = jnp.dot(box, two, preferred_element_type=F32)
    high = sums.astype(BF16)
    low = (sums - high.astype(F32)).astype(BF16)
    for k in range(2):
        rows = slice(row + 64 * k, row + 64 * k + 64)
        for tap in range(9):
            block = (slice(64 * tap, 64 * tap + 64), slice(128 * k, 128 * k + 128))
            columns = slice(128 * tap, 128 * tap + 128)
            high_ref[rows, columns] = high[block]
            low_ref[rows, columns] = low[block]


def most(value):
    return jnp.max(jnp.abs(value).reshape(-1, 8, 128), axis=0)


def edge_kernel(
    count, latent_in, g_in, previous_out, inner_out, outer_out, sems,
):
    core = lax.axis_index("tile") % 2
    inner, outer = 224 * (1 - core), 224 * core
    copies = [
        pltpu.make_async_copy(source, target, sems.at[k])
        for k, (source, target) in enumerate(
            (
                (latent_in.at[pl.ds(count[0] - 2, 2)], previous_out),
                (g_in.at[:, pl.ds(pl.multiple_of(inner, 32), 32)], inner_out),
                (g_in.at[:, pl.ds(pl.multiple_of(outer, 32), 32)], outer_out),
            )
        )
    ]
    for copy in copies:
        copy.start()
    for copy in copies:
        copy.wait()


def weight_kernel(
    count, x_ref, g_ref, previous_ref, inner_ref, outer_ref, box_ref,
    own_ref, sent_ref, high_ref, low_ref, later_ref,
    frames, terms,
):
    used = count[0]
    core = lax.axis_index("tile") % 2
    half, first, second = position()
    frames[:, 0:256] = g_ref[...]
    frames[:, pl.ds(pl.multiple_of(288 - 32 * core, 32), 32)] = inner_ref[...]
    frames[:, pl.ds(pl.multiple_of(256 + 32 * core, 32), 32)] = outer_ref[...]
    for t in range(2, 8):

        @pl.when(t >= used)
        def _():
            frames[t] = jnp.zeros((320, 128), BF16)

    later_ref[...] = frames[0:2]
    for pair in range(4):
        box_sums(
            box_ref[...], frames[2 * pair], frames[2 * pair + 1], high_ref, low_ref, 128 * pair
        )
    peak = [jnp.zeros((8, 128), F32)] * 2
    for dt in range(3):
        parts = [previous_ref[64 * dt :]] if dt < 2 else []
        parts.append(x_ref[: 384 + 64 * dt])
        x = jnp.concatenate(parts, axis=0).T
        for at in range(0, 1152, 256):
            columns = slice(at, min(at + 256, 1152))
            term = jnp.dot(x, high_ref[:, columns], preferred_element_type=F32)
            term = term + jnp.dot(x, low_ref[:, columns], preferred_element_type=F32)
            for k in range(0, term.shape[1], 128):
                tap = 9 * dt + (at + k) // 128
                block = term[:, k : k + 128]
                terms[256 * tap : 256 * tap + 256] = block
                if tap <= 13:
                    peak[0] = jnp.maximum(peak[0], most(block[: 128 if tap == 13 else 256]))
                if tap >= 13:
                    peak[1] = jnp.maximum(peak[1], most(block[128 if tap == 13 else 0 :]))
    for target, which, outer, inner in (
        (own_ref, half, first, second),
        (sent_ref, 1 - half, second, first),
    ):
        for j in range(16):
            start = 3456 * which + 864 * ((j // 4) ^ outer) + 216 * ((j % 4) ^ inner)
            rows = terms[pl.ds(pl.multiple_of(start, 8), 216)]
            target[216 * j : 216 * j + 216] = rows
    low_half = jnp.broadcast_to(jnp.max(peak[0]), (8, 128))
    high_half = jnp.broadcast_to(jnp.max(peak[1]), (8, 128))
    own_ref[3456:3464] = jnp.where(half == 0, low_half, high_half)
    sent_ref[3456:3464] = jnp.where(half == 0, high_half, low_half)


def times_taps(high, low, weight_ref, dt):
    total = None
    for at in range(0, 9, 2):
        taps = range(at, min(at + 2, 9))
        weight = jnp.concatenate([weight_ref[9 * dt + tap] for tap in taps], axis=1)
        columns = slice(128 * at, 128 * at + 128 * len(taps))
        for part in (high, low):
            term = lax.dot_general(
                part[:, columns], weight, (((1,), (1,)), ((), ())), preferred_element_type=F32
            )
            total = term if total is None else total + term
    return total


def input_kernel(weight_ref, high_ref, low_ref, total):
    for dt in (2, 1, 0):
        start = 64 * (2 - dt)
        term = times_taps(high_ref[start:512], low_ref[start:512], weight_ref, dt)
        if start:
            total[0 : 512 - start] += term
        else:
            total[...] = term


def later_kernel(
    count, weight_ref, box_ref, later_ref, before_ref, grad_ref, later_high, later_low, total
):
    used = count[0]
    total[...] = before_ref[...]
    box_sums(box_ref[...], later_ref[0], later_ref[1], later_high, later_low, 0)
    two = pl.ds(pl.multiple_of(64 * used - 128, 64), 128)
    total[two] += times_taps(later_high[...], later_low[...], weight_ref, 0)
    one = pl.ds(pl.multiple_of(64 * used - 64, 64), 64)
    total[one] += times_taps(later_high[0:64], later_low[0:64], weight_ref, 1)
    slot = lax.broadcasted_iota(jnp.int32, (512, 256), 0) // 64
    grad_ref[...] = jnp.where(slot < used, total[...], F32(0)).astype(BF16)


def store_kernel(other, *refs):
    pieces, (out, sems) = refs[:4], refs[-2:]
    half, first, second = position()
    half, place = (1 - half, second) if other else (half, first)
    copies = [
        pltpu.make_async_copy(piece, out.at[half, place ^ step], sems.at[step])
        for step, piece in zip(ORDER, pieces)
    ]
    for copy in copies:
        copy.start()
    for copy in copies:
        copy.wait()


def stored(pieces, before=None):
    far = pl.BlockSpec(memory_space=pltpu.HBM)
    near = pl.BlockSpec(memory_space=pltpu.VMEM)
    other = before is not None
    return pl.pallas_call(
        functools.partial(store_kernel, other),
        out_shape=jax.ShapeDtypeStruct((2, 4, 4, 216, 128), F32),
        in_specs=[near] * 4 + [far] * other,
        out_specs=far,
        scratch_shapes=[pltpu.SemaphoreType.DMA((4,))],
        input_output_aliases={4: 0} if other else {},
        compiler_params=pltpu.CompilerParams(vmem_limit_bytes=24 * 2**20),
        cost_estimate=pl.CostEstimate(flops=0, bytes_accessed=4 * 10**6, transcendentals=0),
    )(*pieces, *([before] if other else []))


def shards(activations, grad_output, conv_weight, frame_counts):
    latent = activations.reshape(8, 64, 256)
    cotangent = grad_output.reshape(8, 256, 128)
    far = pl.BlockSpec(memory_space=pltpu.HBM)
    near = pl.BlockSpec(memory_space=pltpu.VMEM)
    scalars = pl.BlockSpec(memory_space=pltpu.SMEM)
    params = pltpu.CompilerParams(vmem_limit_bytes=24 * 2**20)
    dma = pltpu.SemaphoreType.DMA
    with jax.named_scope("edges"):
        previous, inner, outer = pl.pallas_call(
            edge_kernel,
            out_shape=(
                jax.ShapeDtypeStruct((2, 64, 256), BF16),
                jax.ShapeDtypeStruct((8, 32, 128), BF16),
                jax.ShapeDtypeStruct((8, 32, 128), BF16),
            ),
            in_specs=[scalars] + [far] * 2,
            out_specs=(near,) * 3,
            scratch_shapes=[dma((3,))],
            compiler_params=pltpu.CompilerParams(vmem_limit_bytes=24 * 2**20),
        )(frame_counts, latent, cotangent)
        previous = shifted(previous, 1, 0).reshape(128, 256)
        inner = swapped(inner, "core")
        outer = swapped(outer, "strip")
    with jax.named_scope("box"):
        box = pl.pallas_call(
            box_matrix,
            out_shape=jax.ShapeDtypeStruct((576, 320), BF16),
            out_specs=near,
            compiler_params=params,
            cost_estimate=pl.CostEstimate(
                flops=10**8, bytes_accessed=4 * 10**5, transcendentals=0
            ),
        )()
    with jax.named_scope("weight_terms"):
        own, sent, high, low, later = pl.pallas_call(
            weight_kernel,
            out_shape=(
                jax.ShapeDtypeStruct((3464, 128), F32),
                jax.ShapeDtypeStruct((3464, 128), F32),
                jax.ShapeDtypeStruct((512, 1152), BF16),
                jax.ShapeDtypeStruct((512, 1152), BF16),
                jax.ShapeDtypeStruct((2, 320, 128), BF16),
            ),
            in_specs=[scalars] + [near] * 6,
            out_specs=(near,) * 5,
            scratch_shapes=[
                pltpu.VMEM((8, 320, 128), BF16),
                pltpu.VMEM((6912, 128), F32),
            ],
            compiler_params=params,
            cost_estimate=pl.CostEstimate(
                flops=3 * 10**9, bytes_accessed=10**7, transcendentals=0
            ),
        )(frame_counts, latent.reshape(512, 256), cotangent, previous, inner, outer, box)
    with jax.named_scope("halves"):
        exponent = fitting(sent[3456:3457])
        received = swapped(packed(sent[:3456], exponent, power(exponent)), "core")
        later = shifted(later, -1, 0)
    with jax.named_scope("input_terms"):
        partial = pl.pallas_call(
            input_kernel,
            out_shape=jax.ShapeDtypeStruct((512, 256), F32),
            in_specs=[near] * 3,
            out_specs=near,
            compiler_params=params,
            cost_estimate=pl.CostEstimate(
                flops=2 * 10**9, bytes_accessed=5 * 10**6, transcendentals=0
            ),
        )(conv_weight, high, low)
    with jax.named_scope("later"):

        def finished(partial):
            return pl.pallas_call(
                later_kernel,
                out_shape=jax.ShapeDtypeStruct((512, 256), BF16),
                in_specs=[scalars] + [near] * 4,
                out_specs=near,
                scratch_shapes=[
                    pltpu.VMEM((128, 1152), BF16),
                    pltpu.VMEM((128, 1152), BF16),
                    pltpu.VMEM((512, 256), F32),
                ],
                compiler_params=params,
                cost_estimate=pl.CostEstimate(
                    flops=5 * 10**8, bytes_accessed=10**6, transcendentals=0
                ),
            )(frame_counts, conv_weight, box, later, partial)

    with jax.named_scope("weight_sum"):
        factor = 1.0 / math.sqrt(16 * 16 * 2048)
        grad_weight, grad_input = summed_everywhere(own, received, partial, finished, factor)
    return grad_input.reshape(8, 4, 16, 256), grad_weight.reshape(27, 256, 128)


def solution(mesh):
    placed = (P("tm", "tile", None, None), P("tm", "tile", None, None), P(), P("tm"))
    return jax.shard_map(
        shards,
        mesh=mesh,
        in_specs=placed,
        out_specs=(P("tm", "tile", None, None), P()),
        check_vma=False,
    )
```
